32 devices in a mesh: batch: 8 (over z, x), tensor: 4 (over y, core).
Axes of the slice: x: 2, y: 2, z: 4, core: 2. Of those that a mesh axis runs over, the one named last changes fastest.
Arguments:
- fresh_hidden_state: bfloat16 [256, 3, 8192], P('batch', None, 'tensor'), may hold values from -6 to 6
- base_query_rows: bfloat16 [256, 3, 8192], P('batch', None, 'tensor'), may hold values from -8 to 8
- fresh_key_rows: bfloat16 [256, 3, 1024], P('batch', None, 'tensor'), may hold values from -6 to 6
- fresh_value_rows: bfloat16 [256, 3, 1024], P('batch', None, 'tensor'), may hold values from -12 to 12
- context_key_cache: bfloat16 [256, 64, 1024], P('batch', None, 'tensor'), may hold values from -6 to 6
- context_value_cache: bfloat16 [256, 64, 1024], P('batch', None, 'tensor'), may hold values from -12 to 12
- document_key_rows: bfloat16 [16, 512, 1024], P('batch', None, 'tensor'), may hold values from -6 to 6
- document_value_rows: bfloat16 [16, 512, 1024], P('batch', None, 'tensor'), may hold values from -12 to 12
- adapter_down_panel: bfloat16 [16, 64, 8192], P('batch', None, 'tensor'), may hold values from -0.0625 to 0.0625
- adapter_up_panel: bfloat16 [16, 64, 8192], P('batch', None, 'tensor'), may hold values from -0.75 to 0.75
- tenant_owner_batch: int32 [256, 1], P('batch'), may hold values from 0 to 7; in each aligned block of 32 rows (0 to 31, 32 to 63, ...) at most 8 rows name the same one
- tenant_local_index: int32 [256], P('batch'), may hold values from 0 to 1
- document_block_count: int32 [16], P('batch'), may hold values from 1 to 4, as said below
Outputs:
- attention: bfloat16 [256, 3, 8192], P('batch', None, 'tensor')
The draws below stay inside these ranges and needn't reach their ends.
Inputs may be any that keep to these rules, and one draw needn't show every extreme that they name: `tenant_owner_batch`: among the 32 requests of one index of batch, at most 8 name the same owner, and in every draw some owner is named by exactly 8 of them. `document_block_count`: some tenant's document has exactly 4 blocks.
All inputs are finite; a program needn't handle non-finite values.
Results may differ from the reference program's by a relative error of at most 0.0064.
Values may be sent and summed in bfloat16 or wider, within the bound.
A program may use at most 128 MiB of HBM per device.

```python
import math
import jax
import jax.numpy as jnp
import numpy as np
from jax import lax

MODEL_WIDTH = 8192
QUERY_HEADS = 64
KEY_VALUE_HEADS = 8
HEAD_SIZE = 128
ADAPTER_RANK = 64
TEN_DEV = 2
REQ_DEV = 32
CONTEXT_TOKENS = 64
DOC_BLOCK = 128
DOC_BLOCKS = 4
DECODE_STEPS = 3
DOCUMENT_SLOTS = 512
TENANT_TOTAL = 16
REQUEST_TOTAL = 256
CAP = 8
N_BATCH = 8


def draw_base_query_rows(key, part):
    shape_every_dim = (REQUEST_TOTAL, DECODE_STEPS, QUERY_HEADS * HEAD_SIZE)
    result = jnp.clip(jax.random.normal(key, shape_every_dim, jnp.float32), -6.0, 6.0)
    return result.astype(jnp.bfloat16)


def drawn_keys(key, leading_dims, length_value):
    shape_every_dim = (leading_dims, length_value, KEY_VALUE_HEADS * HEAD_SIZE)
    result = jnp.clip(jax.random.normal(key, shape_every_dim, jnp.float32), -6.0, 6.0)
    return result.astype(jnp.bfloat16)


def draw_document_key_rows(key, part):
    return drawn_keys(key, TENANT_TOTAL, DOCUMENT_SLOTS)


def draw_context_key_cache(key, part):
    return drawn_keys(key, REQUEST_TOTAL, CONTEXT_TOKENS)


def draw_document_block_count(key, part):
    first_key, second_key = jax.random.split(jax.random.fold_in(key, 11))
    counts = jax.random.randint(first_key, (TENANT_TOTAL,), 1, DOC_BLOCKS + 1)
    spot_index = jax.random.randint(second_key, (), 0, TENANT_TOTAL)
    return counts.at[spot_index].set(DOC_BLOCKS).astype(jnp.int32)


def plant(drawn, stream_key, low, largest):
    longest = drawn.shape.index(max(drawn.shape))
    spots = []
    for shift in (0, 1):
        where = [jax.random.randint(jax.random.fold_in(stream_key, axis), (), 0, length) for axis, length in enumerate(drawn.shape)]
        where[longest] = (where[longest] + shift) % drawn.shape[longest]
        spots.append(tuple(where))
    return drawn.at[spots[0]].set(low).at[spots[1]].set(largest)


def shard_levels(own_key, shape, shards, low, largest):
    gain, own = 1.0, jax.random.fold_in(own_key, 6)
    for position, shards_of in shards:
        draws = jnp.exp(jax.random.uniform(jax.random.fold_in(own, position), (shards_of,), jnp.float32, low / len(shards), largest / len(shards)))
        gain = gain * jnp.repeat(draws, shape[position] // shards_of).reshape([-1 if axis == position else 1 for axis in range(len(shape))])
    return gain


def assign_block(rng, own, number, rows, number_of, top, bound, skew):
    sequence = jax.random.permutation(rng, number_of)
    crowded, ordinary = load_shares(number_of, rows * top, bound, skew, True), load_shares(number_of, rows * top, bound, skew, False)
    places = jnp.arange(number_of)

    def named(tallies, rotation):
        used = int((tallies > 0).sum())
        fixed = max(1, used // 4)
        passed = fixed + (places - fixed + rotation * (used - fixed)) % max(1, number_of - fixed)
        return jnp.zeros((number_of,), jnp.int32).at[sequence[jnp.where(places < fixed, places, passed)]].set(jnp.asarray(tallies, jnp.int32))

    tallies = jnp.where(number % 4 == 0, named(crowded, number // 4), named(ordinary, number - number // 4 - 1))
    mixed = jax.random.permutation(jax.random.fold_in(own, 3), number_of)
    source_of, receiver = mixed[0:number_of // 2 * 2:2], mixed[1:number_of // 2 * 2:2]
    slack = jnp.minimum(tallies[source_of] - 1, bound - tallies[receiver]) // 2
    slack = jnp.where((source_of == sequence[0]) | (receiver == sequence[0]) | (tallies[receiver] == 0), 0, jnp.maximum(slack, 0))
    passed = jax.random.randint(jax.random.fold_in(own, 4), (number_of // 2,), 0, 1 << 20) % (slack + 1)
    tallies = tallies.at[source_of].add(-passed).at[receiver].add(passed)
    labels = jnp.searchsorted(jnp.cumsum(tallies), jnp.arange(rows * top), side="right").astype(jnp.int32)
    table = labels.reshape(top, rows).T
    table = table[jax.random.permutation(jax.random.fold_in(own, 1), rows)]
    rotation = jax.random.randint(jax.random.fold_in(own, 2), (rows, 1), 0, top)
    return jnp.take_along_axis(table, (jnp.arange(top)[None, :] + rotation) % top, axis=1)


def load_shares(amount, total, bound, lean, full):
    loads = [(1 << 20) // math.isqrt(grade ** lean) + 1 for grade in range(1, amount + 1)]
    largest = bound if full else min(bound, max(-(-total // amount), total * loads[0] // sum(loads)))
    least = 1 if total - largest >= amount - 1 else 0
    given, rest = [largest] + [least] * (amount - 1), total - largest - least * (amount - 1)
    while rest > 0:
        free = [i for i in range(1, amount) if given[i] < largest] or [i for i in range(1, amount) if given[i] < bound]
        whole, budget = sum([loads[i] for i in free]), rest
        for i in free:
            addition = min(bound - given[i], max(1, budget * loads[i] // whole), rest)
            given[i] = given[i] + addition
            rest = rest - addition
    return np.array(given)


def noise(stream_key, shape, width, reach, cuts=(), kind=jnp.bfloat16):
    drawn = width * jax.random.normal(stream_key, shape, jnp.float32)
    if cuts:
        drawn = drawn * shard_levels(stream_key, shape, cuts, -0.22, 0.18)
    return jnp.clip(drawn, -reach, reach).astype(kind)


def setup_inputs(seed: int = 0) -> dict:
    key_of = jax.random.split(jax.random.key(seed), 14)
    fresh_hidden_state = noise(key_of[0], (REQUEST_TOTAL, DECODE_STEPS, MODEL_WIDTH), 1.0, 6.0, ((0, 8), (2, 4)))
    base_query_rows = draw_base_query_rows(jax.random.fold_in(key_of[13], 71), 0)
    fresh_key_rows = noise(key_of[2], (REQUEST_TOTAL, DECODE_STEPS, KEY_VALUE_HEADS * HEAD_SIZE), 1.0, 6.0, ((0, 8), (2, 4)))
    fresh_value_rows = noise(key_of[3], (REQUEST_TOTAL, DECODE_STEPS, KEY_VALUE_HEADS * HEAD_SIZE), 3.0, 12.0, ((0, 8), (2, 4)))
    context_key_cache = draw_context_key_cache(jax.random.fold_in(key_of[13], 71), 0)
    context_value_cache = noise(key_of[5], (REQUEST_TOTAL, CONTEXT_TOKENS, KEY_VALUE_HEADS * HEAD_SIZE), 3.0, 12.0, ((0, 8), (2, 4)))
    document_key_rows = draw_document_key_rows(jax.random.fold_in(key_of[13], 71), 0)
    document_value_rows = noise(key_of[7], (TENANT_TOTAL, DOCUMENT_SLOTS, KEY_VALUE_HEADS * HEAD_SIZE), 3.0, 12.0, ((0, 8), (2, 4)))
    adapter_down_panel = noise(key_of[8], (TENANT_TOTAL, ADAPTER_RANK, MODEL_WIDTH), MODEL_WIDTH ** -0.5, 0.0625, ((0, 8), (2, 4)))
    adapter_up_panel = noise(key_of[9], (TENANT_TOTAL, ADAPTER_RANK, QUERY_HEADS * HEAD_SIZE), ADAPTER_RANK ** -0.5, 0.75, ((0, 8), (2, 4)))
    tenant_owner_batch_keys = jax.random.split(jax.random.fold_in(key_of[10], 1), REQUEST_TOTAL // REQ_DEV)
    tenant_owner_batch_turns = jax.random.permutation(jax.random.fold_in(key_of[10], 3), REQUEST_TOTAL // REQ_DEV)
    tenant_owner_batch = jax.vmap(lambda own, number: assign_block(jax.random.fold_in(key_of[10], 2), own, number, REQ_DEV, N_BATCH, 1, CAP, 2))(tenant_owner_batch_keys, tenant_owner_batch_turns).reshape((REQUEST_TOTAL, 1))
    tenant_local_index = plant(jax.random.randint(key_of[11], (REQUEST_TOTAL,), 0, TEN_DEV), jax.random.fold_in(key_of[11], 1), 0, TEN_DEV - 1).astype(jnp.int32)
    document_block_count = draw_document_block_count(jax.random.fold_in(key_of[13], 71), 0)
    return dict(fresh_hidden_state=fresh_hidden_state, base_query_rows=base_query_rows, fresh_key_rows=fresh_key_rows, fresh_value_rows=fresh_value_rows, context_key_cache=context_key_cache, context_value_cache=context_value_cache, document_key_rows=document_key_rows, document_value_rows=document_value_rows, adapter_down_panel=adapter_down_panel, adapter_up_panel=adapter_up_panel, tenant_owner_batch=tenant_owner_batch, tenant_local_index=tenant_local_index, document_block_count=document_block_count)


def partial_attention(query_rows_list, key_rows_list, value_rows_list, is_open):
    row_total_count = query_rows_list.shape[0]
    key_total_count = key_rows_list.shape[1]
    query_head_rows = query_rows_list.astype(jnp.float32).reshape(row_total_count, KEY_VALUE_HEADS, QUERY_HEADS // KEY_VALUE_HEADS, HEAD_SIZE)
    key_head_rows = key_rows_list.astype(jnp.float32).reshape(row_total_count, key_total_count, KEY_VALUE_HEADS, HEAD_SIZE)
    value_head_rows = value_rows_list.astype(jnp.float32).reshape(row_total_count, key_total_count, KEY_VALUE_HEADS, HEAD_SIZE)
    scores = jnp.einsum('nkgd,nmkd->nkgm', query_head_rows, key_head_rows) * (HEAD_SIZE ** -0.5)
    scores = jnp.where(is_open[:, None, None, :], scores, -jnp.inf)
    row_peak = jnp.max(scores, axis=-1)
    weights = jnp.exp(scores - row_peak[..., None]).astype(jnp.bfloat16)
    row_total = jnp.sum(weights.astype(jnp.float32), axis=-1)
    mixed_out = jnp.einsum('nkgm,nmkd->nkgd', weights.astype(jnp.float32), value_head_rows)
    return mixed_out.reshape(row_total_count, QUERY_HEADS * HEAD_SIZE), row_peak.reshape(row_total_count, QUERY_HEADS), row_total.reshape(row_total_count, QUERY_HEADS)


def combine(doc_part, own_part):
    doc_out, doc_peak, doc_total = doc_part
    own_out, own_peak, own_total = own_part
    row_total_count = doc_out.shape[0]
    joint = jnp.maximum(doc_peak, own_peak)
    doc_scale = jnp.exp(doc_peak - joint)
    own_scale = jnp.exp(own_peak - joint)
    numer = doc_out.reshape(row_total_count, QUERY_HEADS, HEAD_SIZE) * doc_scale[..., None] + own_out.reshape(row_total_count, QUERY_HEADS, HEAD_SIZE) * own_scale[..., None]
    denom = doc_total * doc_scale + own_total * own_scale
    return (numer / denom[..., None]).reshape(row_total_count, QUERY_HEADS * HEAD_SIZE).astype(jnp.bfloat16)


def reference(fresh_hidden_state, base_query_rows, fresh_key_rows, fresh_value_rows, context_key_cache, context_value_cache, document_key_rows, document_value_rows, adapter_down_panel, adapter_up_panel, tenant_owner_batch, tenant_local_index, document_block_count):
    tenant_of = (tenant_owner_batch[:, 0] * TEN_DEV + tenant_local_index).astype(jnp.int32)
    block_count = REQUEST_TOTAL // REQ_DEV

    def to_blocks(array_in):
        return array_in.reshape((block_count, REQ_DEV) + array_in.shape[1:])

    def per_block(inputs):
        x_blk, query_base_block, kn_blk, vn_blk, ck_blk, cv_blk, tenant_block_rows = inputs
        down_panel_chosen = adapter_down_panel[tenant_block_rows].astype(jnp.float32)
        up_panel_chosen = adapter_up_panel[tenant_block_rows].astype(jnp.float32)
        doc_k = document_key_rows[tenant_block_rows]
        doc_v = document_value_rows[tenant_block_rows]
        doc_open = jnp.arange(DOCUMENT_SLOTS)[None, :] < (DOC_BLOCK * document_block_count[tenant_block_rows])[:, None]
        keys_all = jnp.concatenate([ck_blk, kn_blk], axis=1)
        values_all = jnp.concatenate([cv_blk, vn_blk], axis=1)
        outputs = []
        for decode_step_index in range(DECODE_STEPS):
            rank_projection = jnp.einsum('nd,nrd->nr', x_blk[:, decode_step_index].astype(jnp.float32), down_panel_chosen).astype(jnp.bfloat16)
            adapter_query_delta = jnp.einsum('fm,fmz->fz', rank_projection.astype(jnp.float32), up_panel_chosen)
            query_rows_list = (query_base_block[:, decode_step_index].astype(jnp.float32) + adapter_query_delta).astype(jnp.bfloat16)
            doc_part = partial_attention(query_rows_list, doc_k, doc_v, doc_open)
            own_open = jnp.broadcast_to(jnp.arange(CONTEXT_TOKENS + DECODE_STEPS)[None, :] < CONTEXT_TOKENS + decode_step_index + 1, (REQ_DEV, CONTEXT_TOKENS + DECODE_STEPS))
            own_part = partial_attention(query_rows_list, keys_all, values_all, own_open)
            outputs.append(combine(doc_part, own_part))
        return jnp.stack(outputs, axis=1)

    stacked = lax.map(per_block, (to_blocks(fresh_hidden_state), to_blocks(base_query_rows), to_blocks(fresh_key_rows), to_blocks(fresh_value_rows), to_blocks(context_key_cache), to_blocks(context_value_cache), to_blocks(tenant_of)))
    return stacked.reshape(REQUEST_TOTAL, DECODE_STEPS, QUERY_HEADS * HEAD_SIZE)
```

```python
import functools

import jax
import jax.numpy as jnp
from jax import lax
from jax.experimental import pallas as pl
from jax.experimental.pallas import tpu as pltpu
from jax.sharding import PartitionSpec as P

HEAD = 128
DOC_BLOCK = 128
LOG2E = 1.4426950408889634
LOW = -1e30
GROUP = 8
MESH = pl.DeviceIdType.MESH
F32 = jnp.float32
BF16 = jnp.bfloat16


def iota(shape, axis):
    return lax.broadcasted_iota(jnp.int32, shape, axis)


def split_index(index, size, count):
    high = jnp.zeros_like(index)
    for k in range(1, count):
        high = high + (index >= k * size).astype(jnp.int32)
    return high, index - high * size


def dot(a, b):
    return jnp.dot(a, b, preferred_element_type=F32)


def dot_nt(a, b):
    return lax.dot_general(a, b, (((1,), (1,)), ((), ())), preferred_element_type=F32)


def kernel(
    n, tn, cap, rows,
    x_ref, b_ref, fk_ref, fv_ref, own_ref, loc_ref, cnt_ref,
    ck_hbm, cv_hbm, dk_hbm, dv_hbm, down_hbm, up_hbm,
    out_ref,
    ck, cv, dk, dv, down, up,
    sx, rx, sb, rb, sq, rq, so, ro, part,
    delta, bias, lse, qh, own_out, own_lse,
    in_sem, x_s, x_r, b_s, b_r, q_s, q_r, o_s, o_r, p_s, p_r,
):
    steps, reqs, width = x_ref.shape
    cols = b_ref.shape[2]
    heads = cols // HEAD
    kvs = fk_ref.shape[2] // HEAD
    per_kv = heads // kvs
    tenants, doc_len, _ = dk.shape
    rank = down.shape[1]
    ctx = ck.shape[1]
    total = n * rows
    home = steps * reqs
    half = cols // kvs
    scale = LOG2E * HEAD ** -0.5
    me = lax.axis_index("batch")
    mt = lax.axis_index("tensor")

    barrier = pltpu.get_barrier_semaphore()

    @pl.loop(1, n)
    def _(i):
        pl.semaphore_signal(barrier, inc=1, device_id={"batch": lax.rem(me + i, n)}, device_id_type=MESH)

    for i in range(1, tn):
        pl.semaphore_signal(barrier, inc=1, device_id={"tensor": lax.rem(mt + i, tn)}, device_id_type=MESH)

    loads = [
        pltpu.make_async_copy(src, dst, in_sem.at[k])
        for k, (src, dst) in enumerate(
            [(down_hbm, down), (up_hbm, up), (dk_hbm, dk), (dv_hbm, dv), (ck_hbm, ck), (cv_hbm, cv)]
        )
    ]
    for load in loads:
        load.start()

    owner_col = own_ref[...]
    wide_step, wide_req = split_index(iota((reqs, home), 1), reqs, steps)
    sub = iota((reqs, home), 0)
    owner_wide = jnp.sum(jnp.where(sub == wide_req, owner_col, 0), axis=0, keepdims=True)
    rank_wide = jnp.sum(
        jnp.where((owner_wide == owner_col) & (sub < wide_req), 1, 0), axis=0, keepdims=True
    )
    row_step, row_slot = split_index(iota((rows, home), 0), cap, steps + 1)
    row_hit = (row_step == wide_step[:1]) & (row_slot == rank_wide)
    pack = jnp.concatenate(
        [jnp.where(row_hit & (owner_wide == o), 1.0, 0.0) for o in range(n)], axis=0
    ).astype(BF16)

    tenant_tall = jnp.concatenate(
        [jnp.broadcast_to(loc_ref[...].astype(F32), (reqs, HEAD))] * steps, axis=0
    ).astype(BF16)
    x_all = x_ref[...].reshape(home, width)
    sx[:, :, width:] = dot(pack, tenant_tall).reshape(n, rows, HEAD).astype(BF16)
    for c in range(0, width, 512):
        sx[:, :, c : c + 512] = dot(pack, x_all[:, c : c + 512]).reshape(n, rows, 512).astype(BF16)

    def copy(src, dst, ssem, rsem, i):
        to = lax.rem(me + i, n)
        return pltpu.make_async_remote_copy(
            src_ref=src.at[to], dst_ref=dst.at[me], send_sem=ssem.at[i], recv_sem=rsem.at[i],
            device_id={"batch": to}, device_id_type=MESH,
        )

    def landed(src, dst, ssem, rsem, i):
        come = lax.rem(me - i + n, n)
        pltpu.make_async_remote_copy(
            src_ref=src.at[come], dst_ref=dst.at[come], send_sem=ssem.at[i], recv_sem=rsem.at[i],
            device_id={"batch": come}, device_id_type=MESH,
        ).wait_recv()
        return come

    def start_all(*refs):
        @pl.loop(1, n)
        def _(i):
            copy(*refs, i).start()

    def wait_all(*refs):
        @pl.loop(1, n)
        def _(i):
            landed(*refs, i)

    def sent_all(*refs):
        @pl.loop(1, n)
        def _(i):
            copy(*refs, i).wait_send()

    def stacked(ref, lo, size):
        return jnp.concatenate(
            [ref[j, :, lo : lo + size].astype(F32) for j in range(n)], axis=0
        )

    pl.semaphore_wait(barrier, n - 1 + tn - 1)
    start_all(sx, rx, x_s, x_r)
    rx[me] = sx[me]

    b_all = b_ref[...].reshape(home, cols)
    for c in range(0, cols, 512):
        sb[:, :, c : c + 512] = dot(pack, b_all[:, c : c + 512]).reshape(n, rows, 512).astype(BF16)
    start_all(sb, rb, b_s, b_r)
    rb[me] = sb[me]

    loads[0].wait()
    wait_all(sx, rx, x_s, x_r)
    tenant_rows = stacked(rx, width, HEAD)
    low = jnp.zeros((total, tenants * rank), F32)
    for c in range(0, width, 512):
        low = low + dot_nt(
            stacked(rx, c, 512).astype(BF16), down[:, :, c : c + 512].reshape(tenants * rank, 512)
        )
    lane_tenant, _ = split_index(iota((total, tenants * rank), 1), rank, tenants)
    part[mt] = jnp.where(lane_tenant == tenant_rows[:, :1].astype(jnp.int32), low, 0.0)

    def part_copy(i):
        to = lax.rem(mt + i, tn)
        return pltpu.make_async_remote_copy(
            src_ref=part.at[mt], dst_ref=part.at[mt], send_sem=p_s.at[i], recv_sem=p_r.at[i],
            device_id={"tensor": to}, device_id_type=MESH,
        )

    for i in range(1, tn):
        part_copy(i).start()

    key = iota((total, doc_len), 1)
    for t in range(tenants):
        sees = (tenant_rows[:, :1] == float(t)) & (key < DOC_BLOCK * cnt_ref[t])
        bias[:, t * doc_len : (t + 1) * doc_len] = jnp.where(sees, 0.0, LOW)
    lse[...] = jnp.zeros_like(lse)

    loads[1].wait()
    for i in range(1, tn):
        come = lax.rem(mt - i + tn, tn)
        pltpu.make_async_remote_copy(
            src_ref=part.at[come], dst_ref=part.at[come], send_sem=p_s.at[i], recv_sem=p_r.at[i],
            device_id={"tensor": come}, device_id_type=MESH,
        ).wait_recv()
    spread = part[0]
    for i in range(1, tn):
        spread = spread + part[i]
    spread = spread.astype(BF16)
    for c in range(0, cols, 512):
        delta[:, c : c + 512] = dot(spread, up[:, :, c : c + 512].reshape(tenants * rank, 512))

    def adapt(j):
        here = pl.ds(pl.multiple_of(j * rows, 8), rows)
        q = (rb[j].astype(F32) + delta[here, :]).astype(BF16)
        sq[j] = q
        delta[here, :] = q.astype(F32)

    adapt(me)
    rq[me] = sq[me]

    @pl.loop(1, n)
    def _(i):
        j = landed(sb, rb, b_s, b_r, i)
        adapt(j)
        pltpu.make_async_remote_copy(
            src_ref=sq.at[j], dst_ref=rq.at[me], send_sem=q_s.at[n - i], recv_sem=q_r.at[n - i],
            device_id={"batch": j}, device_id_type=MESH,
        ).start()

    loads[2].wait()
    loads[3].wait()
    lane = iota((total, HEAD), 1)
    _, lane_head = split_index(lane, heads, HEAD // heads)
    for k in range(kvs):
        mine = slice(k * HEAD, (k + 1) * HEAD)

        @pl.loop(0, per_kv)
        def _(g):
            h = k * per_kv + g
            at = pl.ds(pl.multiple_of(h * HEAD, HEAD), HEAD)
            q = delta[:, at].astype(BF16)
            keys = dk[:, :, mine].reshape(tenants * doc_len, HEAD)
            s = dot_nt(q, keys) * scale + bias[...]
            peak = jnp.max(s, axis=1, keepdims=True)
            w = jnp.exp2(s - peak).astype(BF16)
            amount = jnp.sum(w.astype(F32), axis=1, keepdims=True)
            mixed = dot(w, dv[:, :, mine].reshape(tenants * doc_len, HEAD)) / amount
            so[:, :, at] = mixed.reshape(n, rows, HEAD).astype(BF16)
            lse[...] = jnp.where(lane_head == h, peak + jnp.log2(amount), lse[...])

        if k == kvs - 1:
            value = lse[...]
            first = value.astype(BF16).astype(F32)
            second = (value - first).astype(BF16).astype(F32)
            third = value - first - second
            pieces = jnp.where(
                lane < heads, first,
                jnp.where(lane < 2 * heads, second, jnp.where(lane < 3 * heads, third, 0.0)),
            )
            so[:, :, cols:] = pieces.reshape(n, rows, HEAD).astype(BF16)
        lo, size = k * half, half + (HEAD if k == kvs - 1 else 0)
        chunk = (so.at[:, :, lo : lo + size], ro.at[:, :, lo : lo + size], o_s.at[k], o_r.at[k])
        start_all(*chunk)
        ro[me, :, lo : lo + size] = so[me, :, lo : lo + size]

    tall_step, tall_req = split_index(iota((home, total), 0), reqs, steps)
    owner_tall = jnp.concatenate([owner_col] * steps, axis=0)
    rank_col = jnp.sum(
        jnp.where((owner_col == owner_wide[:, :reqs]) & (iota((reqs, reqs), 1) < iota((reqs, reqs), 0)), 1, 0),
        axis=1, keepdims=True,
    )
    rank_tall = jnp.concatenate([rank_col] * steps, axis=0)
    slot_owner, slot_row = split_index(iota((1, total), 1), rows, n)
    unpack = jnp.where(
        (slot_owner == owner_tall) & (slot_row == tall_step * cap + rank_tall), 1.0, 0.0
    ).astype(BF16)
    wait_all(sq, rq, q_s, q_r)
    for c in range(0, cols, 512):
        qh[:, c : c + 512] = dot(unpack, stacked(rq, c, 512).astype(BF16))
    own_lse[...] = jnp.zeros_like(own_lse)
    loads[4].wait()
    loads[5].wait()
    size = per_kv * steps * GROUP
    _, inner = split_index(iota((size, 1), 0), steps * GROUP, per_kv)
    q_step, q_req = split_index(inner, GROUP, steps)
    key_req, _ = split_index(iota((1, GROUP * ctx), 1), ctx, GROUP)
    f_step, f_req = split_index(iota((1, home), 1), reqs, steps)
    ctx_bias = jnp.where(q_req == key_req, 0.0, LOW)
    for g in range(reqs // GROUP):
        fresh_bias = jnp.where((q_req + g * GROUP == f_req) & (f_step <= q_step), 0.0, LOW)
        for k in range(kvs):
            mine = slice(k * HEAD, (k + 1) * HEAD)
            places = [
                (slice(s * reqs + g * GROUP, s * reqs + (g + 1) * GROUP), h)
                for h in range(k * per_kv, (k + 1) * per_kv)
                for s in range(steps)
            ]
            q = jnp.concatenate(
                [qh[r, h * HEAD : (h + 1) * HEAD] for r, h in places], axis=0
            ).astype(BF16)
            keys = ck[g * GROUP : (g + 1) * GROUP, :, mine].reshape(GROUP * ctx, HEAD)
            values = cv[g * GROUP : (g + 1) * GROUP, :, mine].reshape(GROUP * ctx, HEAD)
            sc = dot_nt(q, keys) * scale + ctx_bias
            sf = dot_nt(q, fk_ref[:, :, mine].reshape(home, HEAD)) * scale + fresh_bias
            peak = jnp.maximum(jnp.max(sc, axis=1, keepdims=True), jnp.max(sf, axis=1, keepdims=True))
            wc = jnp.exp2(sc - peak).astype(BF16)
            wf = jnp.exp2(sf - peak).astype(BF16)
            amount = jnp.sum(wc.astype(F32), axis=1, keepdims=True) + jnp.sum(
                wf.astype(F32), axis=1, keepdims=True
            )
            mixed = (dot(wc, values) + dot(wf, fv_ref[:, :, mine].reshape(home, HEAD))) / amount
            level = peak + jnp.log2(amount)
            for e, (r, h) in enumerate(places):
                piece = slice(e * GROUP, (e + 1) * GROUP)
                own_out[r, h * HEAD : (h + 1) * HEAD] = mixed[piece]
                own_lse[r, :] = jnp.where(
                    iota((GROUP, HEAD), 1) == h, level[piece], own_lse[r, :]
                )

    for k in range(kvs):
        lo, size = k * half, half + (HEAD if k == kvs - 1 else 0)
        wait_all(so.at[:, :, lo : lo + size], ro.at[:, :, lo : lo + size], o_s.at[k], o_r.at[k])
    from_piece, from_head = split_index(iota((HEAD, HEAD), 0), heads, HEAD // heads)
    fold = jnp.where(
        (from_head == iota((HEAD, HEAD), 1)) & (from_piece < 3), 1.0, 0.0
    ).astype(BF16)
    doc_lse = dot(dot(unpack, stacked(ro, cols, HEAD).astype(BF16)).astype(BF16), fold)
    top = jnp.maximum(doc_lse, own_lse[...])
    doc_part = jnp.exp2(doc_lse - top)
    own_part = jnp.exp2(own_lse[...] - top)
    alpha = doc_part / (doc_part + own_part)
    for c in range(0, cols, 512):
        doc = dot(unpack, stacked(ro, c, 512).astype(BF16))
        for h in range(c // HEAD, (c + 512) // HEAD):
            own = own_out[:, h * HEAD : (h + 1) * HEAD]
            weight = alpha[:, h : h + 1]
            both = doc[:, h * HEAD - c : (h + 1) * HEAD - c] * weight + own * (1.0 - weight)
            out_ref[:, :, h * HEAD : (h + 1) * HEAD] = both.reshape(steps, reqs, HEAD).astype(BF16)

    sent_all(sx, rx, x_s, x_r)
    sent_all(sb, rb, b_s, b_r)
    sent_all(sq, rq, q_s, q_r)
    for k in range(kvs):
        lo, size = k * half, half + (HEAD if k == kvs - 1 else 0)
        sent_all(so.at[:, :, lo : lo + size], ro.at[:, :, lo : lo + size], o_s.at[k], o_r.at[k])
    for i in range(1, tn):
        part_copy(i).wait_send()


def local(
    fresh_hidden_state,
    base_query_rows,
    fresh_key_rows,
    fresh_value_rows,
    context_key_cache,
    context_value_cache,
    document_key_rows,
    document_value_rows,
    adapter_down_panel,
    adapter_up_panel,
    tenant_owner_batch,
    tenant_local_index,
    document_block_count,
):
    reqs, steps, width = fresh_hidden_state.shape
    cols = base_query_rows.shape[2]
    n = lax.axis_size("batch")
    tn = lax.axis_size("tensor")
    cap = max(2, 2 * reqs // n)
    rows = -(-cap * steps // 8) * 8
    kvs = fresh_key_rows.shape[2] // HEAD
    tenants, rank, _ = adapter_down_panel.shape
    doc_len = document_key_rows.shape[1]
    total = n * rows
    home = reqs * steps
    vmem = pl.BlockSpec(memory_space=pltpu.VMEM)
    smem = pl.BlockSpec(memory_space=pltpu.SMEM)
    hbm = pl.BlockSpec(memory_space=pl.ANY)
    dma = pltpu.SemaphoreType.DMA
    out = pl.pallas_call(
        functools.partial(kernel, n, tn, cap, rows),
        out_shape=jax.ShapeDtypeStruct((steps, reqs, cols), BF16),
        in_specs=[vmem] * 6 + [smem] + [hbm] * 6,
        out_specs=vmem,
        scratch_shapes=[
            pltpu.VMEM(a.shape, BF16)
            for a in (
                context_key_cache, context_value_cache, document_key_rows,
                document_value_rows, adapter_down_panel, adapter_up_panel,
            )
        ]
        + [pltpu.VMEM((n, rows, width + HEAD), BF16)] * 2
        + [pltpu.VMEM((n, rows, cols), BF16)] * 4
        + [pltpu.VMEM((n, rows, cols + HEAD), BF16)] * 2
        + [
            pltpu.VMEM((tn, total, tenants * rank), F32),
            pltpu.VMEM((total, cols), F32),
            pltpu.VMEM((total, tenants * doc_len), F32),
            pltpu.VMEM((total, HEAD), F32),
            pltpu.VMEM((home, cols), F32),
            pltpu.VMEM((home, cols), F32),
            pltpu.VMEM((home, HEAD), F32),
            dma((6,)),
        ]
        + [dma((n,))] * 6
        + [dma((kvs, n))] * 2
        + [dma((tn,))] * 2,
        compiler_params=pltpu.CompilerParams(
            collective_id=0, has_side_effects=True, vmem_limit_bytes=56 * 2**20
        ),
    )(
        fresh_hidden_state.transpose(1, 0, 2),
        base_query_rows.transpose(1, 0, 2),
        fresh_key_rows.transpose(1, 0, 2),
        fresh_value_rows.transpose(1, 0, 2),
        tenant_owner_batch,
        tenant_local_index[:, None],
        document_block_count,
        context_key_cache,
        context_value_cache,
        document_key_rows,
        document_value_rows,
        adapter_down_panel,
        adapter_up_panel,
    )
    return out.transpose(1, 0, 2)


def solution(mesh):
    cut = P("batch", None, "tensor")
    placed = (cut,) * 10 + (P("batch", None), P("batch"), P("batch"))
    return jax.shard_map(local, mesh=mesh, in_specs=placed, out_specs=cut, check_vma=False)
```

```python
import functools

import jax
import jax.numpy as jnp
from jax import lax
from jax.experimental import pallas as pl
from jax.experimental.pallas import tpu as pltpu
from jax.sharding import PartitionSpec as P

HEAD = 128
DOC_BLOCK = 128
LOG2E = 1.4426950408889634
LOW = -1e30
GROUP = 8
CHUNK = 4
MESH = pl.DeviceIdType.MESH
F32 = jnp.float32
BF16 = jnp.bfloat16


def iota(shape, axis):
    return lax.broadcasted_iota(jnp.int32, shape, axis)


def split_index(index, size, count):
    high = jnp.zeros_like(index)
    for k in range(1, count):
        high = high + (index >= k * size).astype(jnp.int32)
    return high, index - high * size


def dot(a, b):
    return jnp.dot(a, b, preferred_element_type=F32)


def dot_nt(a, b):
    return lax.dot_general(a, b, (((1,), (1,)), ((), ())), preferred_element_type=F32)


def kernel(
    n, tn, cap, rows,
    x_ref, b_ref, fk_ref, fv_ref, own_ref, loc_ref, cnt_ref,
    ck_hbm, cv_hbm, dk_hbm, dv_hbm, down_hbm, up_hbm,
    out_ref,
    ck, cv, dk, dv, down, up,
    sx, rx, sb, rb, sq, rq, so, ro, sl, rl, part,
    delta, bias, lse, qh, own_out, own_lse,
    in_sem, x_s, x_r, b_s, b_r, q_s, q_r, o_s, o_r, l_s, l_r, p_s, p_r,
):
    steps, reqs, width = x_ref.shape
    cols = b_ref.shape[2]
    heads = cols // HEAD
    kvs = fk_ref.shape[2] // HEAD
    per_kv = heads // kvs
    tenants, doc_len, _ = dk.shape
    rank = down.shape[1]
    ctx = ck.shape[1]
    total = n * rows
    home = steps * reqs
    scale = LOG2E * HEAD ** -0.5
    me = lax.axis_index("batch")
    mt = lax.axis_index("tensor")

    def partner(i):
        to, bit = 0, 1
        while bit < n:
            to = to + bit * lax.rem(me // bit + i // bit, 2)
            bit *= 2
        return to

    barrier = pltpu.get_barrier_semaphore()

    @pl.loop(1, n)
    def _(i):
        pl.semaphore_signal(barrier, inc=1, device_id={"batch": partner(i)}, device_id_type=MESH)

    for i in range(1, tn):
        pl.semaphore_signal(barrier, inc=1, device_id={"tensor": lax.rem(mt + i, tn)}, device_id_type=MESH)

    loads = [
        pltpu.make_async_copy(src, dst, in_sem.at[k])
        for k, (src, dst) in enumerate(
            [(down_hbm, down), (up_hbm, up), (dk_hbm, dk), (dv_hbm, dv), (ck_hbm, ck), (cv_hbm, cv)]
        )
    ]
    for load in loads:
        load.start()

    diagonal = iota((reqs, reqs), 0) == iota((reqs, reqs), 1)
    owner_col = jnp.sum(jnp.where(diagonal, own_ref[...], 0), axis=1, keepdims=True)
    tenant_col = jnp.sum(jnp.where(diagonal, loc_ref[...], 0), axis=1, keepdims=True)
    wide_step, wide_req = split_index(iota((reqs, home), 1), reqs, steps)
    sub = iota((reqs, home), 0)
    owner_wide = jnp.sum(jnp.where(sub == wide_req, owner_col, 0), axis=0, keepdims=True)
    rank_wide = jnp.sum(
        jnp.where((owner_wide == owner_col) & (sub < wide_req), 1, 0), axis=0, keepdims=True
    )
    row_step, row_slot = split_index(iota((rows, home), 0), cap, steps + 1)
    row_hit = (row_step == wide_step[:1]) & (row_slot == rank_wide)
    pack = jnp.concatenate(
        [jnp.where(row_hit & (owner_wide == o), 1.0, 0.0) for o in range(n)], axis=0
    ).astype(BF16)

    tenant_tall = jnp.concatenate(
        [jnp.broadcast_to(tenant_col.astype(F32), (reqs, HEAD))] * steps, axis=0
    ).astype(BF16)
    x_all = x_ref[...].reshape(home, width)
    sx[:, :, width:] = dot(pack, tenant_tall).reshape(n, rows, HEAD).astype(BF16)
    for c in range(0, width, 512):
        sx[:, :, c : c + 512] = dot(pack, x_all[:, c : c + 512]).reshape(n, rows, 512).astype(BF16)

    def copy(src, dst, ssem, rsem, i):
        to = partner(i)
        return pltpu.make_async_remote_copy(
            src_ref=src.at[to], dst_ref=dst.at[me], send_sem=ssem.at[i], recv_sem=rsem.at[i],
            device_id={"batch": to}, device_id_type=MESH,
        )

    def landed(src, dst, ssem, rsem, i):
        come = partner(i)
        pltpu.make_async_remote_copy(
            src_ref=src.at[come], dst_ref=dst.at[come], send_sem=ssem.at[i], recv_sem=rsem.at[i],
            device_id={"batch": come}, device_id_type=MESH,
        ).wait_recv()
        return come

    def start_all(*refs):
        @pl.loop(1, n)
        def _(i):
            copy(*refs, n - i).start()

    def wait_all(*refs):
        @pl.loop(1, n)
        def _(i):
            landed(*refs, n - i)

    def sent_all(*refs):
        @pl.loop(1, n)
        def _(i):
            copy(*refs, n - i).wait_send()

    def stacked(ref, lo, size):
        return jnp.concatenate(
            [ref[j, :, lo : lo + size].astype(F32) for j in range(n)], axis=0
        )

    pl.semaphore_wait(barrier, n - 1 + tn - 1)
    start_all(sx, rx, x_s, x_r)
    rx[me] = sx[me]

    b_all = b_ref[...].reshape(home, cols)
    for c in range(0, cols, 512):
        sb[:, :, c : c + 512] = dot(pack, b_all[:, c : c + 512]).reshape(n, rows, 512).astype(BF16)
    copy(sb, rb, b_s, b_r, n - 1).start()
    rb[me] = sb[me]

    @pl.loop(1, n)
    def _(i):
        copy(sx, rx, x_s, x_r, n - i).wait_send()

        @pl.when(i > 1)
        def _():
            copy(sb, rb, b_s, b_r, n - i).start()

    loads[0].wait()
    wait_all(sx, rx, x_s, x_r)
    tenant_rows = stacked(rx, width, HEAD)
    low = jnp.zeros((total, tenants * rank), F32)
    for c in range(0, width, 512):
        low = low + dot_nt(
            stacked(rx, c, 512).astype(BF16), down[:, :, c : c + 512].reshape(tenants * rank, 512)
        )
    lane_tenant, _ = split_index(iota((total, tenants * rank), 1), rank, tenants)
    part[mt] = jnp.where(lane_tenant == tenant_rows[:, :1].astype(jnp.int32), low, 0.0)

    def part_copy(i):
        to = lax.rem(mt + i, tn)
        return pltpu.make_async_remote_copy(
            src_ref=part.at[mt], dst_ref=part.at[mt], send_sem=p_s.at[i], recv_sem=p_r.at[i],
            device_id={"tensor": to}, device_id_type=MESH,
        )

    for i in range(1, tn):
        part_copy(i).start()

    key = iota((total, doc_len), 1)
    for t in range(tenants):
        sees = (tenant_rows[:, :1] == float(t)) & (key < DOC_BLOCK * cnt_ref[t])
        bias[:, t * doc_len : (t + 1) * doc_len] = jnp.where(sees, 0.0, LOW)
    lse[...] = jnp.zeros_like(lse)

    loads[1].wait()
    for i in range(1, tn):
        come = lax.rem(mt - i + tn, tn)
        pltpu.make_async_remote_copy(
            src_ref=part.at[come], dst_ref=part.at[come], send_sem=p_s.at[i], recv_sem=p_r.at[i],
            device_id={"tensor": come}, device_id_type=MESH,
        ).wait_recv()
    spread = part[0]
    for i in range(1, tn):
        spread = spread + part[i]
    spread = spread.astype(BF16)
    for c in range(0, cols, 512):
        delta[:, c : c + 512] = dot(spread, up[:, :, c : c + 512].reshape(tenants * rank, 512))

    def adapt(j):
        here = pl.ds(pl.multiple_of(j * rows, 8), rows)
        q = (rb[j].astype(F32) + delta[here, :]).astype(BF16)
        sq[j] = q
        delta[here, :] = q.astype(F32)

    adapt(me)
    rq[me] = sq[me]

    @pl.loop(1, n)
    def _(i):
        j = landed(sb, rb, b_s, b_r, n - i)
        adapt(j)
        copy(sq, rq, q_s, q_r, n - i).start()

    loads[2].wait()
    loads[3].wait()
    lane = iota((total, HEAD), 1)
    _, lane_head = split_index(lane, heads, HEAD // heads)
    def chunk(c):
        at = slice(c * CHUNK * HEAD, (c + 1) * CHUNK * HEAD)
        return so.at[:, :, at], ro.at[:, :, at], o_s.at[c], o_r.at[c]

    for c in range(heads // CHUNK):
        k = c * CHUNK // per_kv
        mine = slice(k * HEAD, (k + 1) * HEAD)

        @pl.loop(c * CHUNK, (c + 1) * CHUNK)
        def _(h):
            at = pl.ds(pl.multiple_of(h * HEAD, HEAD), HEAD)
            q = delta[:, at].astype(BF16)
            keys = dk[:, :, mine].reshape(tenants * doc_len, HEAD)
            s = dot_nt(q, keys) * scale + bias[...]
            peak = jnp.max(s, axis=1, keepdims=True)
            w = jnp.exp2(s - peak).astype(BF16)
            amount = jnp.sum(w.astype(F32), axis=1, keepdims=True)
            mixed = dot(w, dv[:, :, mine].reshape(tenants * doc_len, HEAD)) / amount
            so[:, :, at] = mixed.reshape(n, rows, HEAD).astype(BF16)
            lse[...] = jnp.where(lane_head == h, peak + jnp.log2(amount), lse[...])

        if c == heads // CHUNK - 1:
            value = lse[...]
            first = value.astype(BF16).astype(F32)
            second = (value - first).astype(BF16).astype(F32)
            third = value - first - second
            pieces = jnp.where(
                lane < heads, first,
                jnp.where(lane < 2 * heads, second, jnp.where(lane < 3 * heads, third, 0.0)),
            )
            sl[...] = pieces.reshape(n, rows, HEAD).astype(BF16)
            start_all(sl, rl, l_s, l_r)
            rl[me] = sl[me]
        start_all(*chunk(c))
        at = slice(c * CHUNK * HEAD, (c + 1) * CHUNK * HEAD)
        ro[me, :, at] = so[me, :, at]

    tall_step, tall_req = split_index(iota((home, total), 0), reqs, steps)
    owner_tall = jnp.concatenate([owner_col] * steps, axis=0)
    rank_col = jnp.sum(
        jnp.where((owner_col == owner_wide[:, :reqs]) & (iota((reqs, reqs), 1) < iota((reqs, reqs), 0)), 1, 0),
        axis=1, keepdims=True,
    )
    rank_tall = jnp.concatenate([rank_col] * steps, axis=0)
    slot_owner, slot_row = split_index(iota((1, total), 1), rows, n)
    unpack = jnp.where(
        (slot_owner == owner_tall) & (slot_row == tall_step * cap + rank_tall), 1.0, 0.0
    ).astype(BF16)
    wait_all(sq, rq, q_s, q_r)
    for c in range(0, cols, 512):
        qh[:, c : c + 512] = dot(unpack, stacked(rq, c, 512).astype(BF16))
    own_lse[...] = jnp.zeros_like(own_lse)
    loads[4].wait()
    loads[5].wait()
    size = per_kv * steps * GROUP
    _, inner = split_index(iota((size, 1), 0), steps * GROUP, per_kv)
    q_step, q_req = split_index(inner, GROUP, steps)
    key_req, _ = split_index(iota((1, GROUP * ctx), 1), ctx, GROUP)
    f_step, f_req = split_index(iota((1, home), 1), reqs, steps)
    ctx_bias = jnp.where(q_req == key_req, 0.0, LOW)
    for g in range(reqs // GROUP):
        fresh_bias = jnp.where((q_req + g * GROUP == f_req) & (f_step <= q_step), 0.0, LOW)
        for k in range(kvs):
            mine = slice(k * HEAD, (k + 1) * HEAD)
            places = [
                (slice(s * reqs + g * GROUP, s * reqs + (g + 1) * GROUP), h)
                for h in range(k * per_kv, (k + 1) * per_kv)
                for s in range(steps)
            ]
            q = jnp.concatenate(
                [qh[r, h * HEAD : (h + 1) * HEAD] for r, h in places], axis=0
            ).astype(BF16)
            keys = ck[g * GROUP : (g + 1) * GROUP, :, mine].reshape(GROUP * ctx, HEAD)
            values = cv[g * GROUP : (g + 1) * GROUP, :, mine].reshape(GROUP * ctx, HEAD)
            sc = dot_nt(q, keys) * scale + ctx_bias
            sf = dot_nt(q, fk_ref[:, :, mine].reshape(home, HEAD)) * scale + fresh_bias
            peak = jnp.maximum(jnp.max(sc, axis=1, keepdims=True), jnp.max(sf, axis=1, keepdims=True))
            wc = jnp.exp2(sc - peak).astype(BF16)
            wf = jnp.exp2(sf - peak).astype(BF16)
            amount = jnp.sum(wc.astype(F32), axis=1, keepdims=True) + jnp.sum(
                wf.astype(F32), axis=1, keepdims=True
            )
            mixed = (dot(wc, values) + dot(wf, fv_ref[:, :, mine].reshape(home, HEAD))) / amount
            level = peak + jnp.log2(amount)
            for e, (r, h) in enumerate(places):
                piece = slice(e * GROUP, (e + 1) * GROUP)
                own_out[r, h * HEAD : (h + 1) * HEAD] = mixed[piece]
                own_lse[r, :] = jnp.where(
                    iota((GROUP, HEAD), 1) == h, level[piece], own_lse[r, :]
                )

    wait_all(sl, rl, l_s, l_r)
    from_piece, from_head = split_index(iota((HEAD, HEAD), 0), heads, HEAD // heads)
    fold = jnp.where(
        (from_head == iota((HEAD, HEAD), 1)) & (from_piece < 3), 1.0, 0.0
    ).astype(BF16)
    doc_lse = dot(dot(unpack, stacked(rl, 0, HEAD).astype(BF16)).astype(BF16), fold)
    top = jnp.maximum(doc_lse, own_lse[...])
    doc_part = jnp.exp2(doc_lse - top)
    own_part = jnp.exp2(own_lse[...] - top)
    alpha = doc_part / (doc_part + own_part)
    for c in range(heads // CHUNK):
        wait_all(*chunk(c))
        doc = dot(unpack, stacked(ro, c * CHUNK * HEAD, CHUNK * HEAD).astype(BF16))
        for e in range(CHUNK):
            h = c * CHUNK + e
            own = own_out[:, h * HEAD : (h + 1) * HEAD]
            weight = alpha[:, h : h + 1]
            both = doc[:, e * HEAD : (e + 1) * HEAD] * weight + own * (1.0 - weight)
            out_ref[:, :, h * HEAD : (h + 1) * HEAD] = both.reshape(steps, reqs, HEAD).astype(BF16)

    sent_all(sb, rb, b_s, b_r)
    sent_all(sq, rq, q_s, q_r)
    sent_all(sl, rl, l_s, l_r)
    for c in range(heads // CHUNK):
        sent_all(*chunk(c))
    for i in range(1, tn):
        part_copy(i).wait_send()


def local(
    fresh_hidden_state,
    base_query_rows,
    fresh_key_rows,
    fresh_value_rows,
    context_key_cache,
    context_value_cache,
    document_key_rows,
    document_value_rows,
    adapter_down_panel,
    adapter_up_panel,
    tenant_owner_batch,
    tenant_local_index,
    document_block_count,
):
    reqs, steps, width = fresh_hidden_state.shape
    cols = base_query_rows.shape[2]
    n = lax.axis_size("batch")
    tn = lax.axis_size("tensor")
    cap = max(2, 2 * reqs // n)
    rows = -(-cap * steps // 8) * 8
    tenants, rank, _ = adapter_down_panel.shape
    doc_len = document_key_rows.shape[1]
    total = n * rows
    home = reqs * steps
    vmem = pl.BlockSpec(memory_space=pltpu.VMEM)
    smem = pl.BlockSpec(memory_space=pltpu.SMEM)
    hbm = pl.BlockSpec(memory_space=pl.ANY)
    dma = pltpu.SemaphoreType.DMA
    out = pl.pallas_call(
        functools.partial(kernel, n, tn, cap, rows),
        out_shape=jax.ShapeDtypeStruct((steps, reqs, cols), BF16),
        in_specs=[vmem] * 6 + [smem] + [hbm] * 6,
        out_specs=vmem,
        scratch_shapes=[
            pltpu.VMEM(a.shape, BF16)
            for a in (
                context_key_cache, context_value_cache, document_key_rows,
                document_value_rows, adapter_down_panel, adapter_up_panel,
            )
        ]
        + [pltpu.VMEM((n, rows, width + HEAD), BF16)] * 2
        + [pltpu.VMEM((n, rows, cols), BF16)] * 6
        + [pltpu.VMEM((n, rows, HEAD), BF16)] * 2
        + [
            pltpu.VMEM((tn, total, tenants * rank), F32),
            pltpu.VMEM((total, cols), F32),
            pltpu.VMEM((total, tenants * doc_len), F32),
            pltpu.VMEM((total, HEAD), F32),
            pltpu.VMEM((home, cols), F32),
            pltpu.VMEM((home, cols), F32),
            pltpu.VMEM((home, HEAD), F32),
            dma((6,)),
        ]
        + [dma((n,))] * 6
        + [dma((cols // HEAD // CHUNK, n))] * 2
        + [dma((n,))] * 2
        + [dma((tn,))] * 2,
        compiler_params=pltpu.CompilerParams(
            collective_id=0, has_side_effects=True, vmem_limit_bytes=56 * 2**20
        ),
    )(
        fresh_hidden_state.transpose(1, 0, 2),
        base_query_rows.transpose(1, 0, 2),
        fresh_key_rows.transpose(1, 0, 2),
        fresh_value_rows.transpose(1, 0, 2),
        tenant_owner_batch.reshape(1, reqs),
        tenant_local_index.reshape(1, reqs),
        document_block_count,
        context_key_cache,
        context_value_cache,
        document_key_rows,
        document_value_rows,
        adapter_down_panel,
        adapter_up_panel,
    )
    return out.transpose(1, 0, 2)


def solution(mesh):
    cut = P("batch", None, "tensor")
    placed = (cut,) * 10 + (P("batch", None), P("batch"), P("batch"))
    return jax.shard_map(local, mesh=mesh, in_specs=placed, out_specs=cut, check_vma=False)
```

```python
import functools

import jax
import jax.numpy as jnp
from jax import lax
from jax.experimental import pallas as pl
from jax.experimental.pallas import tpu as pltpu
from jax.sharding import PartitionSpec as P

HEAD = 128
DOC_BLOCK = 128
LOG2E = 1.4426950408889634
LOW = -1e30
GROUP = 8
CHUNK = 4
MESH = pl.DeviceIdType.MESH
F32 = jnp.float32
BF16 = jnp.bfloat16


def iota(shape, axis):
    return lax.broadcasted_iota(jnp.int32, shape, axis)


def split_index(index, size, count):
    high = jnp.zeros_like(index)
    for k in range(1, count):
        high = high + (index >= k * size).astype(jnp.int32)
    return high, index - high * size


def dot(a, b):
    return jnp.dot(a, b, preferred_element_type=F32)


def dot_nt(a, b):
    return lax.dot_general(a, b, (((1,), (1,)), ((), ())), preferred_element_type=F32)


def with_ones(values):
    return jnp.concatenate([values, jnp.ones_like(values)], axis=1)


def kernel(
    n, tn, cap, rows,
    x_ref, b_ref, fk_ref, fv_ref, own_ref, loc_ref, cnt_ref,
    ck_hbm, cv_hbm, dk_hbm, dv_hbm, down_hbm, up_hbm,
    out_ref,
    ck, cv, dk, dv, down, up,
    sx, rx, sb, rb, sq, rq, so, ro, sl, rl, part,
    delta, bias, lse, qh, own_out, own_lse,
    in_sem, x_s, x_r, b_s, b_r, q_s, q_r, o_s, o_r, l_s, l_r, p_s, p_r,
):
    steps, reqs, width = x_ref.shape
    cols = b_ref.shape[2]
    heads = cols // HEAD
    kvs = fk_ref.shape[2] // HEAD
    per_kv = heads // kvs
    tenants, doc_len, _ = dk.shape
    rank = down.shape[1]
    ctx = ck.shape[1]
    total = n * rows
    home = steps * reqs
    scale = LOG2E * HEAD ** -0.5
    me = lax.axis_index("batch")
    mt = lax.axis_index("tensor")

    def partner(i):
        to, bit = 0, 1
        while bit < n:
            to = to + bit * lax.rem(me // bit + i // bit, 2)
            bit *= 2
        return to

    barrier = pltpu.get_barrier_semaphore()

    @pl.loop(1, n)
    def _(i):
        pl.semaphore_signal(barrier, inc=1, device_id={"batch": partner(i)}, device_id_type=MESH)

    for i in range(1, tn):
        pl.semaphore_signal(barrier, inc=1, device_id={"tensor": lax.rem(mt + i, tn)}, device_id_type=MESH)

    loads = [
        pltpu.make_async_copy(src, dst, in_sem.at[k])
        for k, (src, dst) in enumerate(
            [(down_hbm, down), (up_hbm, up), (dk_hbm, dk), (dv_hbm, dv), (ck_hbm, ck), (cv_hbm, cv)]
        )
    ]
    for load in loads:
        load.start()

    diagonal = iota((reqs, reqs), 0) == iota((reqs, reqs), 1)
    owner_col = jnp.sum(jnp.where(diagonal, own_ref[...], 0), axis=1, keepdims=True)
    tenant_col = jnp.sum(jnp.where(diagonal, loc_ref[...], 0), axis=1, keepdims=True)
    wide_step, wide_req = split_index(iota((reqs, home), 1), reqs, steps)
    sub = iota((reqs, home), 0)
    owner_wide = jnp.sum(jnp.where(sub == wide_req, owner_col, 0), axis=0, keepdims=True)
    rank_wide = jnp.sum(
        jnp.where((owner_wide == owner_col) & (sub < wide_req), 1, 0), axis=0, keepdims=True
    )
    row_step, row_slot = split_index(iota((rows, home), 0), cap, steps + 1)
    row_hit = (row_step == wide_step[:1]) & (row_slot == rank_wide)
    pack = jnp.concatenate(
        [jnp.where(row_hit & (owner_wide == o), 1.0, 0.0) for o in range(n)], axis=0
    ).astype(BF16)

    tenant_tall = jnp.concatenate(
        [jnp.broadcast_to(tenant_col.astype(F32), (reqs, HEAD))] * steps, axis=0
    ).astype(BF16)
    x_all = x_ref[...].reshape(home, width)
    sx[:, :, width:] = dot(pack, tenant_tall).reshape(n, rows, HEAD).astype(BF16)
    for c in range(0, width, 512):
        sx[:, :, c : c + 512] = dot(pack, x_all[:, c : c + 512]).reshape(n, rows, 512).astype(BF16)

    def copy(src, dst, ssem, rsem, i):
        to = partner(i)
        return pltpu.make_async_remote_copy(
            src_ref=src.at[to], dst_ref=dst.at[me], send_sem=ssem.at[i], recv_sem=rsem.at[i],
            device_id={"batch": to}, device_id_type=MESH,
        )

    def landed(src, dst, ssem, rsem, i):
        come = partner(i)
        pltpu.make_async_remote_copy(
            src_ref=src.at[come], dst_ref=dst.at[come], send_sem=ssem.at[i], recv_sem=rsem.at[i],
            device_id={"batch": come}, device_id_type=MESH,
        ).wait_recv()
        return come

    def start_all(*refs):
        @pl.loop(1, n)
        def _(i):
            copy(*refs, n - i).start()

    def wait_all(*refs):
        @pl.loop(1, n)
        def _(i):
            landed(*refs, n - i)

    def sent_all(*refs):
        @pl.loop(1, n)
        def _(i):
            copy(*refs, n - i).wait_send()

    def stacked(ref, lo, size):
        return jnp.concatenate(
            [ref[j, :, lo : lo + size].astype(F32) for j in range(n)], axis=0
        )

    pl.semaphore_wait(barrier, n - 1 + tn - 1)
    start_all(sx, rx, x_s, x_r)
    rx[me] = sx[me]

    b_all = b_ref[...].reshape(home, cols)
    for c in range(0, cols, 512):
        sb[:, :, c : c + 512] = dot(pack, b_all[:, c : c + 512]).reshape(n, rows, 512).astype(BF16)
    half = cols // kvs

    def part_of(src, dst, ssem, rsem, k):
        at = slice(k * half, (k + 1) * half)
        return src.at[:, :, at], dst.at[:, :, at], ssem.at[k], rsem.at[k]

    base = [part_of(sb, rb, b_s, b_r, k) for k in range(kvs)]
    query = [part_of(sq, rq, q_s, q_r, k) for k in range(kvs)]
    copy(*base[0], n - 1).start()
    rb[me] = sb[me]

    @pl.loop(1, n)
    def _(i):
        copy(sx, rx, x_s, x_r, n - i).wait_send()

        @pl.when(i > 1)
        def _():
            copy(*base[0], n - i).start()

    loads[0].wait()
    wait_all(sx, rx, x_s, x_r)
    tenant_rows = stacked(rx, width, HEAD)
    low = jnp.zeros((total, tenants * rank), F32)
    for c in range(0, width, 512):
        low = low + dot_nt(
            stacked(rx, c, 512).astype(BF16), down[:, :, c : c + 512].reshape(tenants * rank, 512)
        )
    lane_tenant, _ = split_index(iota((total, tenants * rank), 1), rank, tenants)
    part[mt] = jnp.where(lane_tenant == tenant_rows[:, :1].astype(jnp.int32), low, 0.0)

    def part_copy(i):
        to = lax.rem(mt + i, tn)
        return pltpu.make_async_remote_copy(
            src_ref=part.at[mt], dst_ref=part.at[mt], send_sem=p_s.at[i], recv_sem=p_r.at[i],
            device_id={"tensor": to}, device_id_type=MESH,
        )

    for i in range(1, tn):
        part_copy(i).start()

    key = iota((total, doc_len), 1)
    for t in range(tenants):
        sees = (tenant_rows[:, :1] == float(t)) & (key < DOC_BLOCK * cnt_ref[t])
        bias[:, t * doc_len : (t + 1) * doc_len] = jnp.where(sees, 0.0, LOW)
    lse[...] = jnp.zeros_like(lse)

    for k in range(1, kvs):

        @pl.loop(1, n)
        def _(i):
            copy(*base[k - 1], n - i).wait_send()
            copy(*base[k], n - i).start()

    loads[1].wait()
    for i in range(1, tn):
        come = lax.rem(mt - i + tn, tn)
        pltpu.make_async_remote_copy(
            src_ref=part.at[come], dst_ref=part.at[come], send_sem=p_s.at[i], recv_sem=p_r.at[i],
            device_id={"tensor": come}, device_id_type=MESH,
        ).wait_recv()
    spread = part[0]
    for i in range(1, tn):
        spread = spread + part[i]
    spread = spread.astype(BF16)
    for c in range(0, cols, 512):
        delta[:, c : c + 512] = dot(spread, up[:, :, c : c + 512].reshape(tenants * rank, 512))

    def adapt(j, k):
        here, at = pl.ds(pl.multiple_of(j * rows, 8), rows), slice(k * half, (k + 1) * half)
        q = (rb[j, :, at].astype(F32) + delta[here, at]).astype(BF16)
        sq[j, :, at] = q
        delta[here, at] = q.astype(F32)

    def adapt_all(k):
        adapt(me, k)
        rq[me, :, k * half : (k + 1) * half] = sq[me, :, k * half : (k + 1) * half]

        @pl.loop(1, n)
        def _(i):
            j = landed(*base[k], n - i)
            adapt(j, k)
            copy(*query[k], n - i).start()

    loads[2].wait()
    loads[3].wait()
    lane = iota((total, HEAD), 1)
    _, lane_head = split_index(lane, heads, HEAD // heads)
    def chunk(c):
        at = slice(c * CHUNK * HEAD, (c + 1) * CHUNK * HEAD)
        return so.at[:, :, at], ro.at[:, :, at], o_s.at[c], o_r.at[c]

    for c in range(heads // CHUNK):
        k = c * CHUNK // per_kv
        mine = slice(k * HEAD, (k + 1) * HEAD)
        if c * CHUNK % per_kv == 0:
            adapt_all(k)

        def attend(h):
            at = pl.ds(pl.multiple_of(h * HEAD, HEAD), HEAD)
            q = delta[:, at].astype(BF16)
            keys = dk[:, :, mine].reshape(tenants * doc_len, HEAD)
            s = dot_nt(q, keys) * scale + bias[...]
            peak = jnp.max(s, axis=1, keepdims=True)
            w = jnp.exp2(s - peak).astype(BF16)
            mixed = dot(w, with_ones(dv[:, :, mine].reshape(tenants * doc_len, HEAD)))
            amount = mixed[:, HEAD:]
            doc = mixed[:, :HEAD] / amount
            so[:, :, at] = doc.reshape(n, rows, HEAD).astype(BF16)
            lse[...] = jnp.where(lane_head == h, peak + jnp.log2(amount), lse[...])

        @pl.loop(0, CHUNK // 2)
        def _(g):
            attend(c * CHUNK + 2 * g)
            attend(c * CHUNK + 2 * g + 1)

        if c == heads // CHUNK - 1:
            value = lse[...]
            first = value.astype(BF16).astype(F32)
            second = (value - first).astype(BF16).astype(F32)
            third = value - first - second
            pieces = jnp.where(
                lane < heads, first,
                jnp.where(lane < 2 * heads, second, jnp.where(lane < 3 * heads, third, 0.0)),
            )
            sl[...] = pieces.reshape(n, rows, HEAD).astype(BF16)
            start_all(sl, rl, l_s, l_r)
            rl[me] = sl[me]
        start_all(*chunk(c))
        at = slice(c * CHUNK * HEAD, (c + 1) * CHUNK * HEAD)
        ro[me, :, at] = so[me, :, at]

    tall_step, tall_req = split_index(iota((home, total), 0), reqs, steps)
    owner_tall = jnp.concatenate([owner_col] * steps, axis=0)
    rank_col = jnp.sum(
        jnp.where((owner_col == owner_wide[:, :reqs]) & (iota((reqs, reqs), 1) < iota((reqs, reqs), 0)), 1, 0),
        axis=1, keepdims=True,
    )
    rank_tall = jnp.concatenate([rank_col] * steps, axis=0)
    slot_owner, slot_row = split_index(iota((1, total), 1), rows, n)
    unpack = jnp.where(
        (slot_owner == owner_tall) & (slot_row == tall_step * cap + rank_tall), 1.0, 0.0
    ).astype(BF16)
    for k in range(kvs):
        wait_all(*query[k])
    for c in range(0, cols, 512):
        qh[:, c : c + 512] = dot(unpack, stacked(rq, c, 512).astype(BF16))
    own_lse[...] = jnp.zeros_like(own_lse)
    loads[4].wait()
    loads[5].wait()
    size = per_kv * steps * GROUP
    _, inner = split_index(iota((size, 1), 0), steps * GROUP, per_kv)
    q_step, q_req = split_index(inner, GROUP, steps)
    key_req, _ = split_index(iota((1, GROUP * ctx), 1), ctx, GROUP)
    f_step, f_req = split_index(iota((1, home), 1), reqs, steps)
    ctx_bias = jnp.where(q_req == key_req, 0.0, LOW)
    for g in range(reqs // GROUP):
        fresh_bias = jnp.where((q_req + g * GROUP == f_req) & (f_step <= q_step), 0.0, LOW)
        for k in range(kvs):
            mine = slice(k * HEAD, (k + 1) * HEAD)
            places = [
                (slice(s * reqs + g * GROUP, s * reqs + (g + 1) * GROUP), h)
                for h in range(k * per_kv, (k + 1) * per_kv)
                for s in range(steps)
            ]
            q = jnp.concatenate(
                [qh[r, h * HEAD : (h + 1) * HEAD] for r, h in places], axis=0
            ).astype(BF16)
            keys = ck[g * GROUP : (g + 1) * GROUP, :, mine].reshape(GROUP * ctx, HEAD)
            values = cv[g * GROUP : (g + 1) * GROUP, :, mine].reshape(GROUP * ctx, HEAD)
            sc = dot_nt(q, keys) * scale + ctx_bias
            sf = dot_nt(q, fk_ref[:, :, mine].reshape(home, HEAD)) * scale + fresh_bias
            peak = jnp.maximum(jnp.max(sc, axis=1, keepdims=True), jnp.max(sf, axis=1, keepdims=True))
            wc = jnp.exp2(sc - peak).astype(BF16)
            wf = jnp.exp2(sf - peak).astype(BF16)
            fresh_values = fv_ref[:, :, mine].reshape(home, HEAD)
            mixed = dot(wc, with_ones(values)) + dot(wf, with_ones(fresh_values))
            amount = mixed[:, HEAD:]
            level = peak + jnp.log2(amount)
            mixed = mixed[:, :HEAD] / amount
            for e, (r, h) in enumerate(places):
                piece = slice(e * GROUP, (e + 1) * GROUP)
                own_out[r, h * HEAD : (h + 1) * HEAD] = mixed[piece]
                own_lse[r, :] = jnp.where(
                    iota((GROUP, HEAD), 1) == h, level[piece], own_lse[r, :]
                )

    wait_all(sl, rl, l_s, l_r)
    from_piece, from_head = split_index(iota((HEAD, HEAD), 0), heads, HEAD // heads)
    fold = jnp.where(
        (from_head == iota((HEAD, HEAD), 1)) & (from_piece < 3), 1.0, 0.0
    ).astype(BF16)
    doc_lse = dot(dot(unpack, stacked(rl, 0, HEAD).astype(BF16)).astype(BF16), fold)
    top = jnp.maximum(doc_lse, own_lse[...])
    doc_part = jnp.exp2(doc_lse - top)
    own_part = jnp.exp2(own_lse[...] - top)
    alpha = doc_part / (doc_part + own_part)
    for c in range(heads // CHUNK):
        wait_all(*chunk(c))
        doc = dot(unpack, stacked(ro, c * CHUNK * HEAD, CHUNK * HEAD).astype(BF16))
        for e in range(CHUNK):
            h = c * CHUNK + e
            own = own_out[:, h * HEAD : (h + 1) * HEAD]
            weight = alpha[:, h : h + 1]
            both = doc[:, e * HEAD : (e + 1) * HEAD] * weight + own * (1.0 - weight)
            out_ref[:, :, h * HEAD : (h + 1) * HEAD] = both.reshape(steps, reqs, HEAD).astype(BF16)

    sent_all(*base[kvs - 1])
    for k in range(kvs):
        sent_all(*query[k])
    sent_all(sl, rl, l_s, l_r)
    for c in range(heads // CHUNK):
        sent_all(*chunk(c))
    for i in range(1, tn):
        part_copy(i).wait_send()


def local(
    fresh_hidden_state,
    base_query_rows,
    fresh_key_rows,
    fresh_value_rows,
    context_key_cache,
    context_value_cache,
    document_key_rows,
    document_value_rows,
    adapter_down_panel,
    adapter_up_panel,
    tenant_owner_batch,
    tenant_local_index,
    document_block_count,
):
    reqs, steps, width = fresh_hidden_state.shape
    cols = base_query_rows.shape[2]
    n = lax.axis_size("batch")
    tn = lax.axis_size("tensor")
    cap = max(2, 2 * reqs // n)
    rows = -(-cap * steps // 8) * 8
    tenants, rank, _ = adapter_down_panel.shape
    doc_len = document_key_rows.shape[1]
    total = n * rows
    home = reqs * steps
    vmem = pl.BlockSpec(memory_space=pltpu.VMEM)
    smem = pl.BlockSpec(memory_space=pltpu.SMEM)
    hbm = pl.BlockSpec(memory_space=pl.ANY)
    dma = pltpu.SemaphoreType.DMA
    out = pl.pallas_call(
        functools.partial(kernel, n, tn, cap, rows),
        out_shape=jax.ShapeDtypeStruct((steps, reqs, cols), BF16),
        in_specs=[vmem] * 6 + [smem] + [hbm] * 6,
        out_specs=vmem,
        scratch_shapes=[
            pltpu.VMEM(a.shape, BF16)
            for a in (
                context_key_cache, context_value_cache, document_key_rows,
                document_value_rows, adapter_down_panel, adapter_up_panel,
            )
        ]
        + [pltpu.VMEM((n, rows, width + HEAD), BF16)] * 2
        + [pltpu.VMEM((n, rows, cols), BF16)] * 6
        + [pltpu.VMEM((n, rows, HEAD), BF16)] * 2
        + [
            pltpu.VMEM((tn, total, tenants * rank), F32),
            pltpu.VMEM((total, cols), F32),
            pltpu.VMEM((total, tenants * doc_len), F32),
            pltpu.VMEM((total, HEAD), F32),
            pltpu.VMEM((home, cols), F32),
            pltpu.VMEM((home, cols), F32),
            pltpu.VMEM((home, HEAD), F32),
            dma((6,)),
        ]
        + [dma((n,))] * 2
        + [dma((fresh_key_rows.shape[2] // HEAD, n))] * 4
        + [dma((cols // HEAD // CHUNK, n))] * 2
        + [dma((n,))] * 2
        + [dma((tn,))] * 2,
        compiler_params=pltpu.CompilerParams(
            collective_id=0, has_side_effects=True, vmem_limit_bytes=56 * 2**20
        ),
    )(
        fresh_hidden_state.transpose(1, 0, 2),
        base_query_rows.transpose(1, 0, 2),
        fresh_key_rows.transpose(1, 0, 2),
        fresh_value_rows.transpose(1, 0, 2),
        tenant_owner_batch.reshape(1, reqs),
        tenant_local_index.reshape(1, reqs),
        document_block_count,
        context_key_cache,
        context_value_cache,
        document_key_rows,
        document_value_rows,
        adapter_down_panel,
        adapter_up_panel,
    )
    return out.transpose(1, 0, 2)


def solution(mesh):
    cut = P("batch", None, "tensor")
    placed = (cut,) * 10 + (P("batch", None), P("batch"), P("batch"))
    return jax.shard_map(local, mesh=mesh, in_specs=placed, out_specs=cut, check_vma=False)
```
